32 devices in a mesh: dp: 8 (over z, x), tensor: 4 (over y, core).
Axes of the slice: x: 2, y: 2, z: 4, core: 2. Of those that a mesh axis runs over, the one named last changes fastest.
Arguments:
- d_out: bfloat16 [2048, 3072], P('dp'), may hold values from -12 to 12
- gate: bfloat16 [2048, 4096], P('dp', 'tensor'), may hold values from -6 to 6
- up_proj: bfloat16 [2048, 4096], P('dp', 'tensor'), may hold values from -12 to 12
- master: float32 [4096, 3072], P(('tensor', 'dp')), may hold values from -0.09375 to 0.09375
- moment_one: float32 [4096, 3072], P(('tensor', 'dp')), may hold values from -4 to 4
- moment_two: float32 [4096, 3072], P(('tensor', 'dp')), may hold values from 0.05 to 2
Outputs:
- gate_grad: bfloat16 [2048, 4096], P('dp', 'tensor')
- up_grad: bfloat16 [2048, 4096], P('dp', 'tensor')
- master_next: float32 [4096, 3072], P(('tensor', 'dp'))
- moment_one_next: float32 [4096, 3072], P(('tensor', 'dp'))
- moment_two_next: float32 [4096, 3072], P(('tensor', 'dp'))
- weight_next: bfloat16 [4096, 3072], P('tensor')
The draws below stay inside these ranges and needn't reach their ends.
All inputs are finite; a program needn't handle non-finite values.
Results may differ from the reference program's by a relative error of at most 0.005.
Values may be sent and summed in bfloat16 or wider, within the bound.
No kernel may reach another device: no remote copies, remote signals or barrier semaphores. Data moves between devices by JAX's collectives and lax.ppermute only.
A program may use at most 64 MiB of HBM per device.

```python
import math
import jax
import jax.numpy as jnp

D = 3072
FF = 4096
TOKENS = 2048


def draw_d_out(key, part):
    key_cols, key_base = jax.random.split(key, 2)
    scales = jnp.exp(jax.random.uniform(key_cols, (D,), jnp.float32, jnp.log(0.3), jnp.log(3.0)))
    values = jax.random.normal(key_base, (TOKENS, D), jnp.float32) * scales
    return jnp.clip(values, -12.0, 12.0).astype(jnp.bfloat16)


def draw_up_proj(key, part):
    key_cols, key_base = jax.random.split(key, 2)
    place = jnp.arange(FF, dtype=jnp.float32) / FF
    scales = jnp.exp(jax.random.uniform(key_cols, (FF,), jnp.float32, jnp.log(0.5), jnp.log(1.6)))
    ramp = jnp.sqrt(1.0 + 2.0 * place)
    base = jax.random.normal(key_base, (TOKENS, FF), jnp.float32)
    return jnp.clip(base * scales * ramp, -12.0, 12.0).astype(jnp.bfloat16)


def strengthened(values, key, source, target, parts, factor):
    owner, partner = [(jnp.arange(values.shape[dim]) // (values.shape[dim] // parts)).reshape([-1 if axis == dim else 1 for axis in range(values.ndim)]) for dim in (source, target)]
    chosen = jax.random.permutation(key, parts)[partner]
    strong = (owner == chosen) | (owner == (partner + parts // 2) % parts)
    return jnp.where(strong, factor * values, values)


def levels(rng, dims, pieces, least, largest):
    def one(axis_at, blocks):
        draws = jax.random.uniform(jax.random.fold_in(jax.random.fold_in(rng, 6), axis_at), (blocks,), jnp.float32, least / len(pieces), largest / len(pieces))
        return jnp.repeat(jnp.exp(draws), dims[axis_at] // blocks).reshape((-1,) + (1,) * (len(dims) - axis_at - 1))

    loudness = one(*pieces[0])
    for cut in pieces[1:]:
        loudness = loudness * one(*cut)
    return loudness


def noise(stream_key, dims, deviation, bound, shards=(), kind=jnp.bfloat16):
    loudness = levels(stream_key, dims, shards, -0.22, 0.18) if shards else 1.0
    drawn = jax.random.normal(stream_key, dims, jnp.float32) * deviation * loudness
    return jnp.minimum(jnp.maximum(drawn, -bound), bound).astype(kind)


def bell_draw_with(stream_key, extent, deviation, bound, cuts, heavy, kind=jnp.bfloat16):
    result = deviation * jax.random.normal(stream_key, extent, jnp.float32)
    if cuts:
        result = result * levels(stream_key, extent, cuts, -0.22, 0.18)
    return jnp.clip(strengthened(result, jax.random.fold_in(stream_key, 3), *heavy), -bound, bound).astype(kind)


def setup_inputs(seed: int = 0) -> dict:
    arg_keys = jax.random.split(jax.random.key(seed), 7)
    return {
        "d_out": draw_d_out(jax.random.fold_in(arg_keys[6], 71), 0),
        "gate": bell_draw_with(arg_keys[1], (TOKENS, FF), 1.0, 6.0, ((0, 8), (1, 4)), (0, 1, 8, 2.0)),
        "up_proj": draw_up_proj(jax.random.fold_in(arg_keys[6], 71), 0),
        "master": noise(arg_keys[3], (FF, D), FF ** -0.5, 0.09375, ((0, 32),), jnp.float32),
        "moment_one": noise(arg_keys[4], (FF, D), 0.5, 4.0, ((0, 32),), jnp.float32),
        "moment_two": jnp.clip(jnp.exp(math.log(2.0) - 3.6888794 * jax.random.uniform(arg_keys[5], (FF, D), jnp.float32) ** levels(arg_keys[5], (FF, D), ((0, 32),), -0.2, 0.2)), 0.05, 2.0),
    }


def reference(d_out, gate, up_proj, master, moment_one, moment_two):
    weight = master.astype(jnp.bfloat16)
    gate_f = gate.astype(jnp.float32)
    up_f = up_proj.astype(jnp.float32)
    silu_gate = jax.nn.silu(gate_f)
    hidden = (silu_gate * up_f).astype(jnp.bfloat16)
    d_hidden = jnp.dot(d_out, weight.T, preferred_element_type=jnp.float32)
    up_grad = (d_hidden * silu_gate).astype(jnp.bfloat16)
    sigm = jax.nn.sigmoid(gate_f)
    gate_grad = (d_hidden * up_f * sigm * (1.0 + gate_f * (1.0 - sigm))).astype(jnp.bfloat16)
    grad = jnp.dot(hidden.T, d_out, preferred_element_type=jnp.float32)
    total = jnp.sum(grad * grad)
    factor = 1.0 / jnp.sqrt(total / (FF * D) + 1e-06)
    clipped = grad * factor
    moment_one_next = 0.9 * moment_one + 0.1 * clipped
    moment_two_next = 0.95 * moment_two + 0.05 * clipped * clipped
    master_next = master - 0.003 * (moment_one_next / (jnp.sqrt(moment_two_next) + 1e-08) + 0.1 * master)
    weight_next = master_next.astype(jnp.bfloat16)
    return (gate_grad, up_grad, master_next, moment_one_next, moment_two_next, weight_next)
```

```python
import jax
import jax.numpy as jnp
from jax import lax
from jax.sharding import PartitionSpec as P

D = 3072
FF = 4096
CELL = 8
BF16 = jnp.bfloat16
F32 = jnp.float32

ENDS, MIDS, ALL = (0, 3), (1, 2), (0, 1, 2, 3)
NEIGHBOURS = ((0, 1), (1, 0), (2, 3), (3, 2))
MIDDLE = ((1, 2), (2, 1))
INWARD = ((0, 1), (3, 2))
OUTWARD = ((1, 0), (2, 3))


def on_device(n, d_out, gate, up_proj, master, moment_one, moment_two):
    outer = n // CELL
    place = lax.axis_index("dp")
    z, x = place % CELL // 2, place % 2
    t = lax.axis_index("tensor")
    tokens, width = gate.shape
    rows = master.shape[0]
    part = width // CELL
    cols = D // 4
    ends = (z == 0) | (z == 3)
    same_pair = [[k + CELL * j for j in range(outer)] for k in range(CELL)]

    def line(value, moves):
        return lax.ppermute(
            value,
            "dp",
            [(i, i - i % CELL + b * 2 + i % 2) for i in range(n) for a, b in moves if i % CELL // 2 == a],
        )

    def line_xor(value, m):
        return lax.ppermute(value, "dp", [(i, i ^ (2 * m)) for i in range(n)])

    def pair(value, where):
        return lax.ppermute(value, "dp", [(i, i ^ 1) for i in range(n) if i % CELL // 2 in where])

    def swap(value, m):
        return lax.ppermute(value, "tensor", [(i, i ^ m) for i in range(4)])

    def gather_cell(own):
        size = own.shape[0]
        half = size // 2
        near = line(own, NEIGHBOURS)
        mid = line(own, MIDDLE)
        own_x = pair(own, ALL)
        mid_far = line(near, MIDDLE)
        end_far = line(mid, OUTWARD)
        near_x_mid = line(own_x, INWARD)
        near_x_end = pair(near, ENDS)
        mid_x = pair(mid, MIDS)
        end_last = line(mid_far, OUTWARD)
        end_far_x = pair(end_far, ENDS)
        mid_far_x = pair(mid_far, MIDS)
        last_x_low = pair(end_last[:half], ENDS)
        last_x_high = line(mid_far_x[half:], OUTWARD)
        out = jnp.zeros((CELL * size,) + own.shape[1:], own.dtype)

        def put(out, value, at_z, at_x, shift=0):
            return lax.dynamic_update_slice(out, value, ((at_z * 2 + at_x) * size + shift, 0))

        third = jnp.where(z < 2, 2, 1)
        fourth = jnp.where(z < 2, 3, 0)
        out = put(out, own, z, x)
        out = put(out, own_x, z, 1 - x)
        out = put(out, near, z ^ 1, x)
        out = put(out, jnp.where(ends, near_x_end, near_x_mid), z ^ 1, 1 - x)
        out = put(out, jnp.where(ends, end_far, mid), third, x)
        out = put(out, jnp.where(ends, end_far_x, mid_x), third, 1 - x)
        out = put(out, jnp.where(ends, end_last, mid_far), fourth, x)
        out = put(out, jnp.where(ends, last_x_low, mid_far_x[:half]), fourth, 1 - x)
        return put(out, jnp.where(ends, last_x_high, mid_far_x[half:]), fourth, 1 - x, half)

    d_out_all = gather_cell(lax.dynamic_slice(d_out, (0, t * cols), (tokens, cols)))

    weight = master.astype(BF16)
    if outer > 1:
        weight = lax.all_gather(weight, "dp", axis=0, tiled=True, axis_index_groups=same_pair)
    weight_cols = [
        lax.dynamic_slice(weight, (0, (t ^ m) * cols), (part, cols)) for m in range(4)
    ]
    weight_rows = jnp.concatenate(
        [weight_cols[0]] + [swap(weight_cols[m], m) for m in (1, 2, 3)], axis=0
    )

    gate_f = gate.astype(F32)
    up_f = up_proj.astype(F32)
    silu_gate = jax.nn.silu(gate_f)
    hidden = (silu_gate * up_f).astype(BF16)
    hidden = hidden.reshape(tokens, outer, CELL, rows).transpose(2, 0, 1, 3).reshape(4, 2, tokens, part)
    kept = lax.dynamic_index_in_dim(hidden, x, 1, keepdims=False)
    given = lax.dynamic_index_in_dim(hidden, 1 - x, 1, keepdims=False)
    came = pair(given, ALL)
    first = jnp.where(x == 0, kept, came)
    second = jnp.where(x == 0, came, kept)
    both = jnp.concatenate([first, second], axis=1)
    blocks = [lax.dynamic_index_in_dim(both, z ^ m, 0, keepdims=False) for m in range(4)]
    blocks = [blocks[0]] + [line_xor(blocks[m], m) for m in (1, 2, 3)]
    hidden_mine = jnp.zeros((CELL * tokens, part), BF16)
    for m in range(4):
        hidden_mine = lax.dynamic_update_slice(hidden_mine, blocks[m], ((z ^ m) * 2 * tokens, 0))
    hidden_two = jnp.concatenate([hidden_mine, swap(hidden_mine, 2)], axis=1)
    hidden_far = swap(hidden_two, 1)
    grad_here = jnp.concatenate(
        [
            lax.dot_general(h, d_out_all, (((0,), (0,)), ((), ())), preferred_element_type=F32)
            for h in (hidden_two, hidden_far)
        ],
        axis=0,
    ).reshape(4, part, cols)
    if outer > 1:
        grad_here = lax.psum_scatter(
            grad_here.reshape(4, outer, rows, cols),
            "dp",
            scatter_dimension=1,
            axis_index_groups=same_pair,
        )
    total = jnp.broadcast_to(jnp.sum(grad_here * grad_here), (8, 128))
    for m in (1, 2):
        total = total + swap(total, m)
    step = 1
    while step < n:
        total = total + lax.ppermute(total, "dp", [(i, i ^ step) for i in range(n)])
        step *= 2
    total = total[0, 0]

    grad = jnp.zeros((rows, D), F32)
    pieces = (grad_here[0], swap(grad_here[2], 1), swap(grad_here[1], 2), swap(grad_here[3], 3))
    for m in range(4):
        grad = lax.dynamic_update_slice(grad, pieces[m], (0, (t ^ m) * cols))

    factor = 1.0 / jnp.sqrt(total / (FF * D) + 1e-06)
    clipped = grad * factor
    moment_one_next = 0.9 * moment_one + 0.1 * clipped
    moment_two_next = 0.95 * moment_two + 0.05 * clipped * clipped
    master_next = master - 0.003 * (
        moment_one_next / (jnp.sqrt(moment_two_next) + 1e-08) + 0.1 * master
    )
    shard_next = master_next.astype(BF16)
    if outer > 1:
        shard_next = lax.all_gather(shard_next, "dp", axis=0, tiled=True, axis_index_groups=same_pair)
    weight_next = gather_cell(shard_next)
    if outer > 1:
        weight_next = (
            weight_next.reshape(CELL, outer, rows, D).transpose(1, 0, 2, 3).reshape(width, D)
        )

    def d_hidden_part(weight_part):
        return lax.dot_general(
            d_out_all, weight_part, (((1,), (1,)), ((), ())), preferred_element_type=F32
        )

    weight_rows = weight_rows.reshape(4, part, cols)
    keep = d_hidden_part(weight_rows[0::2].reshape(2 * part, cols))
    give = d_hidden_part(weight_rows[1::2].reshape(2 * part, cols))
    keep = keep + swap(give, 1)
    d_mine = (keep[:, :part] + swap(keep[:, part:], 2)).astype(BF16)
    d_mine = d_mine.reshape(4, 2 * tokens, part)
    blocks = [lax.dynamic_index_in_dim(d_mine, z ^ m, 0, keepdims=False) for m in range(4)]
    blocks = [blocks[0]] + [line_xor(blocks[m], m) for m in (1, 2, 3)]
    mine = jnp.zeros((4, 2 * tokens, part), BF16)
    for m in range(4):
        mine = lax.dynamic_update_slice(mine, blocks[m][None], (z ^ m, 0, 0))
    mine = mine.reshape(4, 2, tokens, part)
    kept = lax.dynamic_index_in_dim(mine, x, 1, keepdims=False)
    came = pair(lax.dynamic_index_in_dim(mine, 1 - x, 1, keepdims=False), ALL)
    first = jnp.where(x == 0, kept, came)
    second = jnp.where(x == 0, came, kept)
    d_hidden = jnp.stack([first, second], axis=1)
    d_hidden = (
        d_hidden.reshape(CELL, tokens, outer, rows).transpose(1, 2, 0, 3).reshape(tokens, width)
    ).astype(F32)

    up_grad = (d_hidden * silu_gate).astype(BF16)
    sigm = jax.nn.sigmoid(gate_f)
    gate_grad = (d_hidden * up_f * sigm * (1.0 + gate_f * (1.0 - sigm))).astype(BF16)
    return (gate_grad, up_grad, master_next, moment_one_next, moment_two_next, weight_next)


def solution(mesh):
    n = mesh.shape["dp"]
    placed = (
        P("dp", None),
        P("dp", "tensor"),
        P("dp", "tensor"),
        P(("tensor", "dp"), None),
        P(("tensor", "dp"), None),
        P(("tensor", "dp"), None),
    )
    return jax.shard_map(
        lambda *args: on_device(n, *args),
        mesh=mesh,
        in_specs=placed,
        out_specs=(
            P("dp", "tensor"),
            P("dp", "tensor"),
            P(("tensor", "dp"), None),
            P(("tensor", "dp"), None),
            P(("tensor", "dp"), None),
            P("tensor", None),
        ),
        check_vma=False,
    )
```

```python
import jax
import jax.numpy as jnp
from jax import lax
from jax.experimental import pallas as pl
from jax.experimental.pallas import tpu as pltpu
from jax.sharding import PartitionSpec as P

D = 3072
FF = 4096
CELL = 8
BF16 = jnp.bfloat16
F32 = jnp.float32
SMEM = pl.BlockSpec(memory_space=pltpu.SMEM)
HBM = pl.BlockSpec(memory_space=pltpu.HBM)

def shaped(shape, dtype):
    return jax.ShapeDtypeStruct(shape, dtype)


def call(body, outs, args, flops=0, moved=0, limit=60, after=()):
    args, after = tuple(args), tuple(after)
    n_in, n_out = len(args) - 1, len(outs)

    def kernel(spot, *refs):
        given, refs = refs[:n_in], refs[n_in + len(after) :]
        results, refs = refs[:n_out], refs[n_out:]
        ins, parts, in_sems, out_sems = refs[:n_in], refs[n_in : n_in + n_out], refs[-2], refs[-1]
        loads = [pltpu.make_async_copy(g, v, in_sems.at[i]) for i, (g, v) in enumerate(zip(given, ins))]
        for load in loads:
            load.start()
        waiting, sent = set(range(n_in)), []

        def need(*which):
            for i in which:
                if i in waiting:
                    loads[i].wait()
                    waiting.remove(i)

        def done(o, *index):
            copy = pltpu.make_async_copy(
                parts[o].at[index] if index else parts[o],
                results[o].at[index] if index else results[o],
                out_sems.at[len(sent)],
            )
            copy.start()
            sent.append(copy)

        body(spot, ins, parts, need, done)
        need(*range(n_in))
        for copy in sent:
            copy.wait()

    return pl.pallas_call(
        kernel,
        out_shape=tuple(outs),
        in_specs=[SMEM] + [HBM] * (n_in + len(after)),
        out_specs=(HBM,) * n_out,
        scratch_shapes=[pltpu.VMEM(a.shape, a.dtype) for a in args[1:]]
        + [pltpu.VMEM(o.shape, o.dtype) for o in outs]
        + [pltpu.SemaphoreType.DMA((n_in,)), pltpu.SemaphoreType.DMA((32,))],
        compiler_params=pltpu.CompilerParams(vmem_limit_bytes=limit << 20),
        cost_estimate=pl.CostEstimate(flops=flops, bytes_accessed=moved, transcendentals=0),
    )(*args, *after)


def hidden_body(spot, ins, outs, need, done):
    gate, up = ins
    kept, given = outs
    z, x = spot[0], spot[1]
    part = kept.shape[1]
    need(0, 1)
    for o, out, side in ((1, given, 1 - x), (0, kept, x)):
        for m in range(4):
            cols = pl.ds(pl.multiple_of((2 * (z ^ m) + side) * part, part), part)
            gate_f = gate[:, cols].astype(F32)
            silu = gate_f * (1.0 / (1.0 + jnp.exp(-gate_f)))
            out[m] = (silu * up[:, cols].astype(F32)).T.astype(BF16)
        done(o)


def turn_body(spot, ins, outs, need, done):
    del spot
    kept, came = ins
    need(0, 1)
    for m in (3, 2, 1, 0):
        outs[m][0] = kept[m]
        outs[m][1] = came[m]
        done(m)


def in_pairs(pieces):
    own, own_x, near, near_x, last, last_x, far, low, high = pieces
    return [((i,), lambda p=p: p[...]) for i, p in enumerate((own, own_x, near, near_x))] + [
        ((6,), lambda: far[...]),
        ((7, 8), lambda: jnp.concatenate([low[...], high[...]], axis=0)),
        ((4,), lambda: last[...]),
        ((5,), lambda: last_x[...]),
    ]


def grad_body(spot, ins, outs, need, done):
    del spot
    pieces, hidden, squares = ins[:9], ins[9:], outs[4]
    part = outs[0].shape[0]
    total = None
    for m, (numbers, right) in enumerate(in_pairs(pieces)):
        need(*numbers, *range(9, 13))
        left = jnp.concatenate([h[m // 2, m % 2] for h in hidden], axis=0)
        term = jnp.dot(left, right(), preferred_element_type=F32)
        total = term if total is None else total + term
    for i in (3, 2, 1, 0):
        outs[i][...] = total[i * part : (i + 1) * part].astype(outs[i].dtype)
        done(i)
    squares[...] = jnp.broadcast_to(jnp.sum(total * total), squares.shape)
    done(4)


def d_hidden_body(spot, ins, outs, need, done):
    del spot
    pieces, weights = ins[:9], ins[9:]
    keep, give = outs
    part = weights[0].shape[0]
    tokens = pieces[0].shape[0]
    need(*range(9, 13))
    weight = jnp.concatenate([w[...] for w in weights], axis=0)
    for m, (numbers, side) in enumerate(in_pairs(pieces)):
        need(*numbers)
        out = lax.dot_general(side(), weight, (((1,), (1,)), ((), ())), preferred_element_type=F32)
        rows = slice(m * tokens, (m + 1) * tokens)
        keep[0, rows] = out[:, :part]
        give[0, rows] = out[:, part : 2 * part]
        keep[1, rows] = out[:, 2 * part : 3 * part]
        give[1, rows] = out[:, 3 * part :]
        at = pl.ds(m * tokens, tokens)
        done(0, slice(None), at)
        done(1, slice(None), at)


def add_body(spot, ins, outs, need, done):
    del spot
    keep, give = ins
    mine, sent = outs
    need(0, 1)
    sent[...] = keep[1] + give[1]
    done(1)
    mine[...] = keep[0] + give[0]
    done(0)


def back_body(spot, ins, outs, need, done):
    del spot
    mine, came = ins
    rows = outs[0].shape[0]
    need(0, 1)
    for m in (3, 2, 1, 0):
        at = slice(m * rows, (m + 1) * rows)
        outs[m][...] = (mine[at] + came[at]).astype(BF16)
        done(m)


def adam_body(spot, ins, outs, need, done):
    total, grads = ins[0], ins[1:5]
    master, one, two = ins[5:]
    master_next, one_next, two_next, shard = outs
    t = spot[2]
    cols = grads[0].shape[1]
    need(0)
    factor = 1.0 / jnp.sqrt(total[0:1, 0:1] / (FF * D) + 1e-06)
    need(5, 6, 7)
    for m, g in enumerate(grads):
        need(1 + m)
        at = pl.ds(pl.multiple_of((t ^ m) * cols, cols), cols)
        clipped = g[...].astype(F32) * factor
        first = 0.9 * one[:, at] + 0.1 * clipped
        second = 0.95 * two[:, at] + 0.05 * clipped * clipped
        old = master[:, at]
        new = old - 0.003 * (first / (jnp.sqrt(second) + 1e-08) + 0.1 * old)
        one_next[:, at] = first
        two_next[:, at] = second
        master_next[:, at] = new
        shard[:, at] = new.astype(BF16)
        for o in (3, 0, 1, 2):
            done(o, slice(None), at)


def outputs_body(spot, ins, outs, need, done):
    gate, up, *blocks, came = ins
    gate_grad, up_grad = outs
    z, x = spot[0], spot[1]
    tokens, part = came.shape[1:]
    need(*range(7))
    for m, block in enumerate(blocks):
        for side in range(2):
            d_hidden = (came[m] if side else block[:tokens]).astype(F32)
            cols = pl.ds(pl.multiple_of((2 * (z ^ m) + (x ^ side)) * part, part), part)
            gate_f = gate[:, cols].astype(F32)
            sigm = 1.0 / (1.0 + jnp.exp(-gate_f))
            up_grad[:, cols] = (d_hidden * (gate_f * sigm)).astype(BF16)
            gate_grad[:, cols] = (
                d_hidden * up[:, cols].astype(F32) * sigm * (1.0 + gate_f * (1.0 - sigm))
            ).astype(BF16)
    done(0)
    done(1)


def gate_body(*refs):
    del refs


def together(*values):
    return pl.pallas_call(
        gate_body,
        out_shape=tuple(shaped(v.shape, v.dtype) for v in values),
        in_specs=[HBM] * len(values),
        out_specs=(HBM,) * len(values),
        input_output_aliases={i: i for i in range(len(values))},
        compiler_params=pltpu.CompilerParams(vmem_limit_bytes=60 << 20),
    )(*values)


def on_device(n, d_out, gate, up_proj, master, moment_one, moment_two):
    outer = n // CELL
    place = lax.axis_index("dp")
    z, x = place % CELL // 2, place % 2
    t = lax.axis_index("tensor")
    spot = jnp.stack([z, x, t]).astype(jnp.int32)
    tokens, width = gate.shape
    rows = master.shape[0]
    part = width // CELL
    cols = D // 4
    same_pair = [[k + CELL * j for j in range(outer)] for k in range(CELL)]

    def across(value, m):
        return lax.ppermute(value, "dp", [(i, i ^ m) for i in range(n)])

    def swap(value, m):
        return lax.ppermute(value, "tensor", [(i, i ^ m) for i in range(4)])

    def in_order(pieces):
        own, own_x, near, near_x, last, last_x, far, low, high = pieces
        size, half = own.shape[0], low.shape[0]
        out = jnp.zeros((CELL * size,) + own.shape[1:], own.dtype)
        for value, m, shift in (
            (own, 0, 0), (own_x, 1, 0), (near, 2, 0), (near_x, 3, 0), (last, 6, 0),
            (last_x, 7, 0), (far, 4, 0), (low, 5, 0), (high, 5, half),
        ):
            at = (place % CELL ^ m) * size + shift
            out = lax.dynamic_update_slice(out, value, (at, 0))
        return out

    def by_place(value):
        if outer == 1:
            return value
        return value.reshape(tokens, outer, CELL, rows).transpose(0, 2, 1, 3).reshape(tokens, width)

    gate, up_proj = by_place(gate), by_place(up_proj)

    own = lax.dynamic_slice(d_out, (0, t * cols), (tokens, cols))
    half = tokens // 2
    near, own_x, last = across(own, 2), across(own, 1), across(own, 6)
    block = shaped((4, part, tokens), BF16)
    kept, given = call(hidden_body, (block, block), (spot, gate, up_proj), moved=2 << 20)
    near, own_x, given = together(near, own_x, given)
    near_x, came = across(near, 1), across(given, 1)
    last, came = together(last, came)
    far, last_x = across(last, 2), across(last, 1)
    pair = shaped((2, part, tokens), BF16)
    blocks = call(turn_body, (pair,) * 4, (spot, kept, came), moved=1 << 20)
    blocks = [blocks[0]] + [across(blocks[m], 2 * m) for m in (1, 2, 3)]
    far, last_x, *blocks = together(far, last_x, *blocks)
    low, high = across(far[:half], 1), across(last_x[half:], 2)
    hidden = jnp.stack(blocks)
    hidden_y, hidden_c = swap(hidden, 2), swap(hidden, 1)
    hiddens = (hidden, hidden_c, hidden_y, swap(hidden_y, 1))
    weight = master
    if outer > 1:
        weight = lax.all_gather(
            master.astype(BF16), "dp", axis=0, tiled=True, axis_index_groups=same_pair
        )
    weights = [
        lax.dynamic_slice(weight, (0, (t ^ m) * cols), (part, cols)).astype(BF16) for m in range(4)
    ]
    weights = [weights[0]] + [swap(weights[m], m) for m in (1, 2, 3)]
    pieces = (own, own_x, near, near_x, last, last_x, far, low, high)

    flops = 2 * 4 * part * CELL * tokens * cols
    piece, sent = shaped((part, cols), F32), shaped((part, cols), BF16)
    *grads, total = call(
        grad_body,
        (piece, sent, sent, sent, shaped((8, 128), F32)),
        (spot, *pieces, *hiddens),
        flops=flops,
        moved=8 << 20,
    )
    if outer > 1:
        grads = lax.psum_scatter(
            jnp.stack([g.astype(F32) for g in grads]).reshape(4, outer, rows, cols),
            "dp",
            scatter_dimension=1,
            axis_index_groups=same_pair,
        )
        total = jnp.broadcast_to(jnp.sum(grads * grads), (8, 128))
    grad_own = grads[0]
    step = 1
    while step < n:
        total = total + across(total, step)
        step *= 2
    for m in (1, 2):
        total = total + swap(total, m)
    grads = [grads[0]] + [swap(grads[m], m) for m in (1, 2, 3)]

    sums = shaped((2, CELL * tokens, part), F32)
    keep, give = call(
        d_hidden_body,
        (sums, sums),
        (spot, *pieces, *weights),
        flops=flops,
        moved=10 << 20,
        after=(grad_own,),
    )
    give = swap(give, 1)

    state = shaped((rows, D), F32)
    master_next, moment_one_next, moment_two_next, shard_next = call(
        adam_body,
        (state, state, state, shaped((rows, D), BF16)),
        (spot, total, *grads, master, moment_one, moment_two),
        moved=12 << 20,
    )
    if outer > 1:
        shard_next = lax.all_gather(
            shard_next, "dp", axis=0, tiled=True, axis_index_groups=same_pair
        )
    own = shard_next
    half = own.shape[0] // 2
    near, own_x, last = across(own, 2), across(own, 1), across(own, 6)
    mine_sum = shaped((CELL * tokens, part), F32)
    mine, sent = call(add_body, (mine_sum,) * 2, (spot, keep, give), moved=6 << 20)
    came = swap(sent, 2)
    near, own_x = together(near, own_x)
    near_x = across(near, 1)
    last, near_x = together(last, near_x)
    far, last_x = across(last, 2), across(last, 1)
    pair = shaped((2 * tokens, part), BF16)
    blocks = call(back_body, (pair,) * 4, (spot, mine, came), moved=3 << 20)
    blocks = [blocks[0]] + [across(blocks[m], 2 * m) for m in (1, 2, 3)]
    far, last_x, *blocks = together(far, last_x, *blocks)
    low, high = across(far[:half], 1), across(last_x[half:], 2)
    came = across(jnp.stack([b[tokens:] for b in blocks]), 1)
    out = shaped((tokens, width), BF16)
    gate_grad, up_grad = call(
        outputs_body, (out, out), (spot, gate, up_proj, *blocks, came), moved=4 << 20
    )
    weight_next = in_order((own, own_x, near, near_x, last, last_x, far, low, high))
    if outer > 1:
        weight_next = (
            weight_next.reshape(CELL, outer, rows, D).transpose(1, 0, 2, 3).reshape(width, D)
        )

    def from_place(value):
        if outer == 1:
            return value
        return value.reshape(tokens, CELL, outer, rows).transpose(0, 2, 1, 3).reshape(tokens, width)

    return (
        from_place(gate_grad),
        from_place(up_grad),
        master_next,
        moment_one_next,
        moment_two_next,
        weight_next,
    )


def solution(mesh):
    n = mesh.shape["dp"]
    placed = (
        P("dp", None),
        P("dp", "tensor"),
        P("dp", "tensor"),
        P(("tensor", "dp"), None),
        P(("tensor", "dp"), None),
        P(("tensor", "dp"), None),
    )
    return jax.shard_map(
        lambda *args: on_device(n, *args),
        mesh=mesh,
        in_specs=placed,
        out_specs=(
            P("dp", "tensor"),
            P("dp", "tensor"),
            P(("tensor", "dp"), None),
            P(("tensor", "dp"), None),
            P(("tensor", "dp"), None),
            P("tensor", None),
        ),
        check_vma=False,
    )
```

```python
import jax
import jax.numpy as jnp
from jax import lax
from jax.experimental import pallas as pl
from jax.experimental.pallas import tpu as pltpu
from jax.sharding import PartitionSpec as P

D = 3072
FF = 4096
CELL = 8
BF16 = jnp.bfloat16
F32 = jnp.float32
SMEM = pl.BlockSpec(memory_space=pltpu.SMEM)
HBM = pl.BlockSpec(memory_space=pltpu.HBM)
ANY = pl.BlockSpec(memory_space=pl.ANY)
NEAR = pl.BlockSpec(memory_space=pltpu.VMEM)

MIDDLE = ((1, 2), (2, 1))
ROUND = ((0, 3), (3, 0))


def shaped(shape, dtype):
    return jax.ShapeDtypeStruct(shape, dtype)


class Near:
    def __init__(self, value):
        self.value = value


class Joined:
    def __init__(self, shape, dtype, parts):
        self.shape, self.dtype, self.parts = shape, dtype, parts


def call(body, outs, args, flops=0, moved=0, limit=24, after=()):
    spot, *args = args
    n_in, n_out = len(args), len(outs)
    flat, specs, scratch, todo = [], [], [], []

    def operand(value, spec):
        for i, old in enumerate(flat):
            if old is value and specs[i] is spec:
                return i
        flat.append(value)
        specs.append(spec)
        return len(flat) - 1

    for i, arg in enumerate(args):
        if isinstance(arg, Near):
            todo.append(operand(arg.value, NEAR))
            continue
        scratch.append(pltpu.VMEM(arg.shape, arg.dtype))
        steps = []
        for value, source, target in arg.parts if isinstance(arg, Joined) else ((arg, None, None),):
            steps.append((operand(value, ANY), source, target))
        todo.append(steps)
    count = sum(len(steps) for steps in todo if not isinstance(steps, int))

    def kernel(spot, *refs):
        given, refs = refs[: len(flat)], refs[len(flat) + len(after) :]
        results, refs = refs[:n_out], refs[n_out:]
        slots, parts = list(refs[: len(scratch)]), refs[len(scratch) : len(scratch) + n_out]
        in_sems, out_sems = refs[-2], refs[-1]
        ins, loads, used = [], {}, 0
        for i, steps in enumerate(todo):
            if isinstance(steps, int):
                ins.append(given[steps])
                continue
            ins.append(slots.pop(0))
            loads[i] = []
            for k, source, target in steps:
                copy = pltpu.make_async_copy(
                    given[k] if source is None else given[k].at[source],
                    ins[i] if target is None else ins[i].at[target],
                    in_sems.at[used],
                )
                used += 1
                copy.start()
                loads[i].append(copy)
        sent = []

        def need(*which):
            for i in which:
                for load in loads.pop(i, ()):
                    load.wait()

        def done(o, *index):
            copy = pltpu.make_async_copy(
                parts[o].at[index] if index else parts[o],
                results[o].at[index] if index else results[o],
                out_sems.at[len(sent)],
            )
            copy.start()
            sent.append(copy)

        body(spot, ins, parts, need, done)
        need(*range(n_in))
        for copy in sent:
            copy.wait()

    return pl.pallas_call(
        kernel,
        out_shape=tuple(outs),
        in_specs=[SMEM] + specs + [HBM] * len(after),
        out_specs=(HBM,) * n_out,
        scratch_shapes=scratch
        + [pltpu.VMEM(o.shape, o.dtype) for o in outs]
        + [pltpu.SemaphoreType.DMA((max(1, count),)), pltpu.SemaphoreType.DMA((32,))],
        compiler_params=pltpu.CompilerParams(vmem_limit_bytes=limit << 20),
        cost_estimate=pl.CostEstimate(flops=flops, bytes_accessed=moved, transcendentals=0),
    )(spot, *flat, *after)


def hidden_body(spot, ins, outs, need, done):
    gate, up = ins
    kept, given = outs
    z, x = spot[0], spot[1]
    part = kept.shape[1]
    need(0, 1)
    for o, out, side in ((1, given, 1 - x), (0, kept, x)):
        for m in range(4):
            cols = pl.ds(pl.multiple_of((2 * (z ^ m) + side) * part, part), part)
            gate_f = gate[:, cols].astype(F32)
            silu = gate_f * (1.0 / (1.0 + jnp.exp(-gate_f)))
            out[m] = (silu * up[:, cols].astype(F32)).T.astype(BF16)
        done(o)


def turn_body(spot, ins, outs, need, done):
    del spot
    kept, came = ins
    need(0, 1)
    for m in (3, 2, 1, 0):
        outs[m][0] = kept[m]
        outs[m][1] = came[m]
        done(m)


def tokens_in_rows(pieces):
    size, cols = pieces[0].shape
    parts = []
    for m, piece in enumerate(pieces):
        piece = piece if isinstance(piece, tuple) else (piece,)
        rows = size // len(piece)
        parts += [(p, None, (pl.ds(m * size + i * rows, rows),)) for i, p in enumerate(piece)]
    return Joined((len(pieces) * size, cols), pieces[0].dtype, parts)


def tokens_in_columns(hiddens):
    _, _, part, size = hiddens[0].shape
    parts = []
    for i, h in enumerate(hiddens):
        for m in range(CELL):
            parts.append((h, (m // 2, m % 2), (pl.ds(i * part, part), pl.ds(m * size, size))))
    return Joined((4 * part, CELL * size), hiddens[0].dtype, parts)


def grad_body(spot, ins, outs, need, done):
    del spot
    left, right = ins
    part = outs[0].shape[0]
    need(0, 1)
    total = jnp.dot(left[...], right[...], preferred_element_type=F32)
    for i in (3, 2, 1, 0):
        outs[i][...] = total[i * part : (i + 1) * part].astype(outs[i].dtype)
        done(i)
    outs[4][...] = jnp.broadcast_to(jnp.sum(total * total), outs[4].shape)
    done(4)


def d_hidden_body(spot, ins, outs, need, done):
    del spot
    pieces, weights = ins
    keep, give = outs
    part = weights.shape[0] // 4
    tokens = pieces.shape[0] // CELL
    need(0, 1)
    weight = weights[...].T
    for m in range(CELL):
        at = pl.ds(m * tokens, tokens)
        out = jnp.dot(pieces[at, :], weight, preferred_element_type=F32)
        for i, into in ((1, give), (3, give), (0, keep), (2, keep)):
            into[i // 2, at] = out[:, i * part : (i + 1) * part]
        done(1, slice(None), at)
        done(0, slice(None), at)


def add_body(spot, ins, outs, need, done):
    del spot
    keep, give = ins
    mine, sent = outs
    need(0, 1)
    sent[...] = keep[1] + give[1]
    done(1)
    mine[...] = keep[0] + give[0]
    done(0)


def back_body(spot, ins, outs, need, done):
    del spot
    mine, came = ins
    rows = outs[0].shape[0]
    need(0, 1)
    for m in (3, 2, 1, 0):
        at = slice(m * rows, (m + 1) * rows)
        outs[m][...] = (mine[at] + came[at]).astype(BF16)
        done(m)


def adam_body(spot, ins, outs, need, done):
    total, grads = ins[0], ins[1:5]
    master, one, two = ins[5:]
    master_next, one_next, two_next, shard = outs
    t = spot[2]
    cols = grads[0].shape[1]
    need(0)
    factor = 1.0 / jnp.sqrt(total[0:1, 0:1] / (FF * D) + 1e-06)
    need(5, 6, 7)
    for m, g in enumerate(grads):
        need(1 + m)
        at = pl.ds(pl.multiple_of((t ^ m) * cols, cols), cols)
        clipped = g[...].astype(F32) * factor
        first = 0.9 * one[:, at] + 0.1 * clipped
        second = 0.95 * two[:, at] + 0.05 * clipped * clipped
        old = master[:, at]
        new = old - 0.003 * (first / (jnp.sqrt(second) + 1e-08) + 0.1 * old)
        one_next[:, at] = first
        two_next[:, at] = second
        master_next[:, at] = new
        shard[:, at] = new.astype(BF16)
        for o in (3, 0, 1, 2):
            done(o, slice(None), at)


def outputs_body(spot, ins, outs, need, done):
    gate, up, *blocks, came = ins
    gate_grad, up_grad = outs
    z, x = spot[0], spot[1]
    tokens, part = came.shape[1:]
    need(*range(7))
    for m, block in enumerate(blocks):
        for side in range(2):
            d_hidden = (came[m] if side else block[:tokens]).astype(F32)
            cols = pl.ds(pl.multiple_of((2 * (z ^ m) + (x ^ side)) * part, part), part)
            gate_f = gate[:, cols].astype(F32)
            sigm = 1.0 / (1.0 + jnp.exp(-gate_f))
            up_grad[:, cols] = (d_hidden * (gate_f * sigm)).astype(BF16)
            gate_grad[:, cols] = (
                d_hidden * up[:, cols].astype(F32) * sigm * (1.0 + gate_f * (1.0 - sigm))
            ).astype(BF16)
    done(0)
    done(1)


def gate_body(*refs):
    del refs


def together(*values):
    return pl.pallas_call(
        gate_body,
        out_shape=tuple(shaped(v.shape, v.dtype) for v in values),
        in_specs=[HBM] * len(values),
        out_specs=(HBM,) * len(values),
        input_output_aliases={i: i for i in range(len(values))},
        compiler_params=pltpu.CompilerParams(vmem_limit_bytes=8 << 20),
    )(*values)


def on_device(n, d_out, gate, up_proj, master, moment_one, moment_two):
    outer = n // CELL
    place = lax.axis_index("dp")
    z, x = place % CELL // 2, place % 2
    t = lax.axis_index("tensor")
    spot = jnp.stack([z, x, t]).astype(jnp.int32)
    tokens, width = gate.shape
    rows = master.shape[0]
    part = width // CELL
    cols = D // 4
    same_pair = [[k + CELL * j for j in range(outer)] for k in range(CELL)]

    def across(value, m):
        return lax.ppermute(value, "dp", [(i, i ^ m) for i in range(n)])

    def line(value, pairs):
        steps = [(i, b) for i in range(n) for a, b in pairs if i % CELL // 2 == a]
        return lax.ppermute(value, "dp", [(i, i - i % CELL + b * 2 + i % 2) for i, b in steps])

    def swap(value, m):
        return lax.ppermute(value, "tensor", [(i, i ^ m) for i in range(4)])

    def in_order(pieces):
        own, own_x, near, near_x, last, last_x, far, low, high = pieces
        size, half = own.shape[0], low.shape[0]
        out = jnp.zeros((CELL * size,) + own.shape[1:], own.dtype)
        for value, m, shift in (
            (own, 0, 0), (own_x, 1, 0), (near, 2, 0), (near_x, 3, 0), (last, 6, 0),
            (last_x, 7, 0), (far, 4, 0), (low, 5, 0), (high, 5, half),
        ):
            at = (place % CELL ^ m) * size + shift
            out = lax.dynamic_update_slice(out, value, (at, 0))
        return out

    def by_place(value):
        if outer == 1:
            return value
        return value.reshape(tokens, outer, CELL, rows).transpose(0, 2, 1, 3).reshape(tokens, width)

    gate, up_proj = by_place(gate), by_place(up_proj)

    own = lax.dynamic_slice(d_out, (0, t * cols), (tokens, cols))
    half = tokens // 2
    ends = (z == 0) | (z == 3)
    near, own_x, mid = across(own, 2), across(own, 1), line(own, MIDDLE)
    block = shaped((4, part, tokens), BF16)
    kept, given = call(hidden_body, (block, block), (spot, gate, up_proj), moved=2 << 20)
    near, own_x, mid, given, own = together(near, own_x, mid, given, own)
    end, near_x, came = line(own, ROUND), across(near, 1), across(given, 1)
    end, near_x, came = together(end, near_x, came)
    last = jnp.where(ends, end, mid)
    far, last_x = across(last, 2), across(last, 1)
    pair = shaped((2, part, tokens), BF16)
    blocks = call(turn_body, (pair,) * 4, (spot, kept, came), moved=1 << 20)
    blocks = [blocks[0]] + [across(blocks[m], 2 * m) for m in (1, 2, 3)]
    far, last_x, *blocks = together(far, last_x, *blocks)
    low, high = across(far[:half], 1), across(last_x[half:], 2)
    hidden = jnp.stack(blocks)
    hidden_y, hidden_c = swap(hidden, 2), swap(hidden, 1)
    low, high, hidden_y = together(low, high, hidden_y)
    hiddens = (hidden, hidden_c, hidden_y, swap(hidden_y, 1))
    weight = master
    if outer > 1:
        weight = lax.all_gather(
            master.astype(BF16), "dp", axis=0, tiled=True, axis_index_groups=same_pair
        )
    weights = [
        lax.dynamic_slice(weight, (0, (t ^ m) * cols), (part, cols)).astype(BF16) for m in range(4)
    ]
    weights = [weights[0]] + [swap(weights[m], m) for m in (1, 2, 3)]
    pieces = tokens_in_rows((own, own_x, near, near_x, far, (low, high), last, last_x))

    flops = 2 * 4 * part * CELL * tokens * cols
    piece, sent = shaped((part, cols), F32), shaped((part, cols), BF16)
    *grads, total = call(
        grad_body,
        (piece, sent, sent, sent, shaped((8, 128), F32)),
        (spot, tokens_in_columns(hiddens), pieces),
        flops=flops,
        moved=8 << 20,
        limit=52,
    )
    if outer > 1:
        grads = lax.psum_scatter(
            jnp.stack([g.astype(F32) for g in grads]).reshape(4, outer, rows, cols),
            "dp",
            scatter_dimension=1,
            axis_index_groups=same_pair,
        )
        total = jnp.broadcast_to(jnp.sum(grads * grads), (8, 128))
    grad_own = grads[0]
    step = 1
    while step < n:
        total = total + across(total, step)
        step *= 2
    for m in (1, 2):
        total = total + swap(total, m)
    grads = [grads[0]] + [swap(grads[m], m) for m in (1, 2, 3)]

    sums = shaped((2, CELL * tokens, part), F32)
    weights = Joined(
        (4 * part, cols), BF16, [(w, None, (pl.ds(m * part, part),)) for m, w in enumerate(weights)]
    )
    keep, give = call(
        d_hidden_body,
        (sums, sums),
        (spot, pieces, weights),
        flops=flops,
        moved=10 << 20,
        limit=52,
        after=(grad_own,),
    )
    give = swap(give, 1)

    state = shaped((rows, D), F32)
    master_next, moment_one_next, moment_two_next, shard_next = call(
        adam_body,
        (state, state, state, shaped((rows, D), BF16)),
        (spot, total, *grads, master, moment_one, moment_two),
        moved=12 << 20,
    )
    if outer > 1:
        shard_next = lax.all_gather(
            shard_next, "dp", axis=0, tiled=True, axis_index_groups=same_pair
        )
    own = shard_next
    half = own.shape[0] // 2
    near, own_x, mid = across(own, 2), across(own, 1), line(own, MIDDLE)
    mine_sum = shaped((CELL * tokens, part), F32)
    mine, sent = call(add_body, (mine_sum,) * 2, (spot, keep, give), moved=6 << 20)
    near, own_x, mid, sent, own = together(near, own_x, mid, sent, own)
    end, near_x, came = line(own, ROUND), across(near, 1), swap(sent, 2)
    end, near_x = together(end, near_x)
    last = jnp.where(ends, end, mid)
    far, last_x = across(last, 2), across(last, 1)
    pair = shaped((2 * tokens, part), BF16)
    blocks = call(back_body, (pair,) * 4, (spot, mine, came), moved=3 << 20)
    blocks = [blocks[0]] + [across(blocks[m], 2 * m) for m in (1, 2, 3)]
    far, last_x, *blocks = together(far, last_x, *blocks)
    low, high = across(far[:half], 1), across(last_x[half:], 2)
    came = across(jnp.stack([b[tokens:] for b in blocks]), 1)
    out = shaped((tokens, width), BF16)
    gate_grad, up_grad = call(
        outputs_body, (out, out), (spot, gate, up_proj, *blocks, came), moved=4 << 20
    )
    weight_next = in_order((own, own_x, near, near_x, last, last_x, far, low, high))
    if outer > 1:
        weight_next = (
            weight_next.reshape(CELL, outer, rows, D).transpose(1, 0, 2, 3).reshape(width, D)
        )

    def from_place(value):
        if outer == 1:
            return value
        return value.reshape(tokens, CELL, outer, rows).transpose(0, 2, 1, 3).reshape(tokens, width)

    return (
        from_place(gate_grad),
        from_place(up_grad),
        master_next,
        moment_one_next,
        moment_two_next,
        weight_next,
    )


def solution(mesh):
    n = mesh.shape["dp"]
    placed = (
        P("dp", None),
        P("dp", "tensor"),
        P("dp", "tensor"),
        P(("tensor", "dp"), None),
        P(("tensor", "dp"), None),
        P(("tensor", "dp"), None),
    )
    return jax.shard_map(
        lambda *args: on_device(n, *args),
        mesh=mesh,
        in_specs=placed,
        out_specs=(
            P("dp", "tensor"),
            P("dp", "tensor"),
            P(("tensor", "dp"), None),
            P(("tensor", "dp"), None),
            P(("tensor", "dp"), None),
            P("tensor", None),
        ),
        check_vma=False,
    )
```

```python
import jax
import jax.numpy as jnp
from jax import lax
from jax.experimental import pallas as pl
from jax.experimental.pallas import tpu as pltpu
from jax.sharding import PartitionSpec as P

D = 3072
FF = 4096
CELL = 8
BF16 = jnp.bfloat16
F32 = jnp.float32
SMEM = pl.BlockSpec(memory_space=pltpu.SMEM)
HBM = pl.BlockSpec(memory_space=pltpu.HBM)
ANY = pl.BlockSpec(memory_space=pl.ANY)
NEAR = pl.BlockSpec(memory_space=pltpu.VMEM)

MIDDLE = ((1, 2), (2, 1))
ROUND = ((0, 3), (3, 0))


def shaped(shape, dtype):
    return jax.ShapeDtypeStruct(shape, dtype)


class Near:
    def __init__(self, value):
        self.value = value


class Joined:
    def __init__(self, shape, dtype, parts):
        self.shape, self.dtype, self.parts = shape, dtype, parts


def call(body, outs, args, flops=0, moved=0, limit=24, after=()):
    spot, *args = args
    n_in, n_out = len(args), len(outs)
    flat, specs, scratch, todo = [], [], [], []

    def operand(value, spec):
        for i, old in enumerate(flat):
            if old is value and specs[i] is spec:
                return i
        flat.append(value)
        specs.append(spec)
        return len(flat) - 1

    for i, arg in enumerate(args):
        if isinstance(arg, Near):
            todo.append(operand(arg.value, NEAR))
            continue
        scratch.append(pltpu.VMEM(arg.shape, arg.dtype))
        steps = []
        for value, source, target in arg.parts if isinstance(arg, Joined) else ((arg, None, None),):
            steps.append((operand(value, ANY), source, target))
        todo.append(steps)
    count = sum(len(steps) for steps in todo if not isinstance(steps, int))

    def kernel(spot, *refs):
        given, refs = refs[: len(flat)], refs[len(flat) + len(after) :]
        results, refs = refs[:n_out], refs[n_out:]
        slots, parts = list(refs[: len(scratch)]), refs[len(scratch) : len(scratch) + n_out]
        in_sems, out_sems = refs[-2], refs[-1]
        ins, loads, used = [], {}, 0
        for i, steps in enumerate(todo):
            if isinstance(steps, int):
                ins.append(given[steps])
                continue
            ins.append(slots.pop(0))
            loads[i] = []
            for k, source, target in steps:
                copy = pltpu.make_async_copy(
                    given[k] if source is None else given[k].at[source],
                    ins[i] if target is None else ins[i].at[target],
                    in_sems.at[used],
                )
                used += 1
                copy.start()
                loads[i].append(copy)
        sent = []

        def need(*which):
            for i in which:
                for load in loads.pop(i, ()):
                    load.wait()

        def done(o, *index):
            copy = pltpu.make_async_copy(
                parts[o].at[index] if index else parts[o],
                results[o].at[index] if index else results[o],
                out_sems.at[len(sent)],
            )
            copy.start()
            sent.append(copy)

        body(spot, ins, parts, need, done)
        need(*range(n_in))
        for copy in sent:
            copy.wait()

    return pl.pallas_call(
        kernel,
        out_shape=tuple(outs),
        in_specs=[SMEM] + specs + [HBM] * len(after),
        out_specs=(HBM,) * n_out,
        scratch_shapes=scratch
        + [pltpu.VMEM(o.shape, o.dtype) for o in outs]
        + [pltpu.SemaphoreType.DMA((max(1, count),)), pltpu.SemaphoreType.DMA((32,))],
        compiler_params=pltpu.CompilerParams(vmem_limit_bytes=limit << 20),
        cost_estimate=pl.CostEstimate(flops=flops, bytes_accessed=moved, transcendentals=0),
    )(spot, *flat, *after)


def hidden_body(spot, ins, outs, need, done):
    gate, up = ins
    kept, given = outs
    z, x = spot[0], spot[1]
    part = kept.shape[1]
    need(0, 1)
    for o, out, side in ((1, given, 1 - x), (0, kept, x)):
        for m in range(4):
            cols = pl.ds(pl.multiple_of((2 * (z ^ m) + side) * part, part), part)
            gate_f = gate[:, cols].astype(F32)
            silu = gate_f * (1.0 / (1.0 + jnp.exp(-gate_f)))
            out[m] = (silu * up[:, cols].astype(F32)).T.astype(BF16)
        done(o)


def turn_body(spot, ins, outs, need, done):
    del spot
    kept, came = ins
    need(0, 1)
    for m in (3, 2, 1, 0):
        outs[m][0] = kept[m]
        outs[m][1] = came[m]
        done(m)


def tokens_in_rows(pieces):
    size, cols = pieces[0].shape
    parts = []
    for m, piece in enumerate(pieces):
        piece = piece if isinstance(piece, tuple) else (piece,)
        rows = size // len(piece)
        parts += [(p, None, (pl.ds(m * size + i * rows, rows),)) for i, p in enumerate(piece)]
    return Joined((len(pieces) * size, cols), pieces[0].dtype, parts)


def hidden_blocks(hiddens):
    shape = hiddens[0].shape
    parts = [(h, None, (i,)) for i, h in enumerate(hiddens)]
    return Joined((4,) + shape, hiddens[0].dtype, parts)


def grad_body(spot, ins, outs, need, done):
    del spot
    hidden, pieces = ins
    part, size = hidden.shape[-2:]
    need(0, 1)
    total = None
    for m in range(CELL):
        left = jnp.concatenate([hidden[i, m // 2, m % 2] for i in range(4)], axis=0)
        right = pieces[m * size : (m + 1) * size, :]
        term = jnp.dot(left, right, preferred_element_type=F32)
        total = term if total is None else total + term
    for i in (3, 2, 1, 0):
        outs[i][...] = total[i * part : (i + 1) * part].astype(outs[i].dtype)
        done(i)
    outs[4][...] = jnp.broadcast_to(jnp.sum(total * total), outs[4].shape)
    done(4)


def d_hidden_body(spot, ins, outs, need, done):
    del spot
    pieces, weights = ins
    keep, give = outs
    part = weights.shape[0] // 4
    tokens = pieces.shape[0] // CELL
    need(0, 1)
    weight = weights[...].T
    for m in range(CELL):
        at = pl.ds(m * tokens, tokens)
        out = jnp.dot(pieces[at, :], weight, preferred_element_type=F32)
        for i, into in ((1, give), (3, give), (0, keep), (2, keep)):
            into[i // 2, at] = out[:, i * part : (i + 1) * part]
        done(1, slice(None), at)
        done(0, slice(None), at)


def add_body(spot, ins, outs, need, done):
    del spot
    keep, give = ins
    mine, sent = outs
    need(0, 1)
    sent[...] = keep[1] + give[1]
    done(1)
    mine[...] = keep[0] + give[0]
    done(0)


def back_body(spot, ins, outs, need, done):
    del spot
    mine, came = ins
    rows = outs[0].shape[0]
    need(0, 1)
    for m in (3, 2, 1, 0):
        at = slice(m * rows, (m + 1) * rows)
        outs[m][...] = (mine[at] + came[at]).astype(BF16)
        done(m)


def adam_body(spot, ins, outs, need, done):
    total, grads = ins[0], ins[1:5]
    master, one, two = ins[5:]
    master_next, one_next, two_next, shard = outs
    t = spot[2]
    cols = grads[0].shape[1]
    need(0)
    factor = 1.0 / jnp.sqrt(total[0:1, 0:1] / (FF * D) + 1e-06)
    need(5, 6, 7)
    for m, g in enumerate(grads):
        need(1 + m)
        at = pl.ds(pl.multiple_of((t ^ m) * cols, cols), cols)
        clipped = g[...].astype(F32) * factor
        first = 0.9 * one[:, at] + 0.1 * clipped
        second = 0.95 * two[:, at] + 0.05 * clipped * clipped
        old = master[:, at]
        new = old - 0.003 * (first / (jnp.sqrt(second) + 1e-08) + 0.1 * old)
        one_next[:, at] = first
        two_next[:, at] = second
        master_next[:, at] = new
        shard[:, at] = new.astype(BF16)
        for o in (3, 0, 1, 2):
            done(o, slice(None), at)


def outputs_body(spot, ins, outs, need, done):
    gate, up, *blocks, came = ins
    gate_grad, up_grad = outs
    z, x = spot[0], spot[1]
    tokens, part = came.shape[1:]
    need(*range(7))
    for m, block in enumerate(blocks):
        for side in range(2):
            d_hidden = (came[m] if side else block[:tokens]).astype(F32)
            cols = pl.ds(pl.multiple_of((2 * (z ^ m) + (x ^ side)) * part, part), part)
            gate_f = gate[:, cols].astype(F32)
            sigm = 1.0 / (1.0 + jnp.exp(-gate_f))
            up_grad[:, cols] = (d_hidden * (gate_f * sigm)).astype(BF16)
            gate_grad[:, cols] = (
                d_hidden * up[:, cols].astype(F32) * sigm * (1.0 + gate_f * (1.0 - sigm))
            ).astype(BF16)
    done(0)
    done(1)


def gate_body(*refs):
    del refs


def together(*values, after=()):
    return pl.pallas_call(
        gate_body,
        out_shape=tuple(shaped(v.shape, v.dtype) for v in values),
        in_specs=[HBM] * len(values) + [ANY] * len(after),
        out_specs=(HBM,) * len(values),
        input_output_aliases={i: i for i in range(len(values))},
        compiler_params=pltpu.CompilerParams(vmem_limit_bytes=8 << 20),
    )(*values, *after)


def on_device(n, d_out, gate, up_proj, master, moment_one, moment_two):
    outer = n // CELL
    place = lax.axis_index("dp")
    z, x = place % CELL // 2, place % 2
    t = lax.axis_index("tensor")
    spot = jnp.stack([z, x, t]).astype(jnp.int32)
    tokens, width = gate.shape
    rows = master.shape[0]
    part = width // CELL
    cols = D // 4
    same_pair = [[k + CELL * j for j in range(outer)] for k in range(CELL)]

    def across(value, m):
        return lax.ppermute(value, "dp", [(i, i ^ m) for i in range(n)])

    def line(value, pairs):
        steps = [(i, b) for i in range(n) for a, b in pairs if i % CELL // 2 == a]
        return lax.ppermute(value, "dp", [(i, i - i % CELL + b * 2 + i % 2) for i, b in steps])

    def swap(value, m):
        return lax.ppermute(value, "tensor", [(i, i ^ m) for i in range(4)])

    def in_order(pieces):
        own, own_x, near, near_x, last, last_x, far, low, high = pieces
        size, half = own.shape[0], low.shape[0]
        out = jnp.zeros((CELL * size,) + own.shape[1:], own.dtype)
        for value, m, shift in (
            (own, 0, 0), (own_x, 1, 0), (near, 2, 0), (near_x, 3, 0), (last, 6, 0),
            (last_x, 7, 0), (far, 4, 0), (low, 5, 0), (high, 5, half),
        ):
            at = (place % CELL ^ m) * size + shift
            out = lax.dynamic_update_slice(out, value, (at, 0))
        return out

    def by_place(value):
        if outer == 1:
            return value
        return value.reshape(tokens, outer, CELL, rows).transpose(0, 2, 1, 3).reshape(tokens, width)

    gate, up_proj = by_place(gate), by_place(up_proj)

    own = lax.dynamic_slice(d_out, (0, t * cols), (tokens, cols))
    half = tokens // 2
    ends = (z == 0) | (z == 3)
    near, own_x, mid = across(own, 2), across(own, 1), line(own, MIDDLE)
    block = shaped((4, part, tokens), BF16)
    kept, given = call(hidden_body, (block, block), (spot, gate, up_proj), moved=2 << 20)
    near, own_x, mid, given, own = together(near, own_x, mid, given, own)
    end, near_x, came = line(own, ROUND), across(near, 1), across(given, 1)
    end, came = together(end, came, after=(near_x,))
    last = jnp.where(ends, end, mid)
    far, last_x = across(last, 2), across(last, 1)
    pair = shaped((2, part, tokens), BF16)
    blocks = call(turn_body, (pair,) * 4, (spot, kept, came), moved=1 << 20)
    blocks = [blocks[0]] + [across(blocks[m], 2 * m) for m in (1, 2, 3)]
    far, last_x, *blocks = together(far, last_x, *blocks)
    low, high = across(far[:half], 1), across(last_x[half:], 2)
    hidden = jnp.stack(blocks)
    hidden_y, hidden_c = swap(hidden, 2), swap(hidden, 1)
    (hidden_y,) = together(hidden_y, after=(low, high))
    hiddens = (hidden, hidden_c, hidden_y, swap(hidden_y, 1))
    weight = master
    if outer > 1:
        weight = lax.all_gather(
            master.astype(BF16), "dp", axis=0, tiled=True, axis_index_groups=same_pair
        )
    weights = [
        lax.dynamic_slice(weight, (0, (t ^ m) * cols), (part, cols)).astype(BF16) for m in range(4)
    ]
    weights = [weights[0]] + [swap(weights[m], m) for m in (1, 2, 3)]
    pieces = tokens_in_rows((own, own_x, near, near_x, far, (low, high), last, last_x))

    flops = 2 * 4 * part * CELL * tokens * cols
    piece, sent = shaped((part, cols), F32), shaped((part, cols), BF16)
    *grads, total = call(
        grad_body,
        (piece, sent, sent, sent, shaped((8, 128), F32)),
        (spot, hidden_blocks(hiddens), pieces),
        flops=flops,
        moved=8 << 20,
        limit=52,
    )
    if outer > 1:
        grads = lax.psum_scatter(
            jnp.stack([g.astype(F32) for g in grads]).reshape(4, outer, rows, cols),
            "dp",
            scatter_dimension=1,
            axis_index_groups=same_pair,
        )
        total = jnp.broadcast_to(jnp.sum(grads * grads), (8, 128))
    grad_own = grads[0]
    step = 1
    while step < n:
        total = total + across(total, step)
        step *= 2
    for m in (1, 2):
        total = total + swap(total, m)
    grads = [grads[0]] + [swap(grads[m], m) for m in (1, 2, 3)]

    sums = shaped((2, CELL * tokens, part), F32)
    weights = Joined(
        (4 * part, cols), BF16, [(w, None, (pl.ds(m * part, part),)) for m, w in enumerate(weights)]
    )
    keep, give = call(
        d_hidden_body,
        (sums, sums),
        (spot, pieces, weights),
        flops=flops,
        moved=10 << 20,
        limit=52,
        after=(grad_own,),
    )
    give = swap(give, 1)

    state = shaped((rows, D), F32)
    master_next, moment_one_next, moment_two_next, shard_next = call(
        adam_body,
        (state, state, state, shaped((rows, D), BF16)),
        (spot, total, *grads, master, moment_one, moment_two),
        moved=12 << 20,
    )
    if outer > 1:
        shard_next = lax.all_gather(
            shard_next, "dp", axis=0, tiled=True, axis_index_groups=same_pair
        )
    own = shard_next
    half = own.shape[0] // 2
    near, own_x, mid = across(own, 2), across(own, 1), line(own, MIDDLE)
    mine_sum = shaped((CELL * tokens, part), F32)
    mine, sent = call(add_body, (mine_sum,) * 2, (spot, keep, give), moved=6 << 20)
    near, own_x, mid, sent, own = together(near, own_x, mid, sent, own)
    end, near_x, came = line(own, ROUND), across(near, 1), swap(sent, 2)
    end, near_x = together(end, near_x)
    last = jnp.where(ends, end, mid)
    far, last_x = across(last, 2), across(last, 1)
    pair = shaped((2 * tokens, part), BF16)
    blocks = call(back_body, (pair,) * 4, (spot, mine, came), moved=3 << 20)
    blocks = [blocks[0]] + [across(blocks[m], 2 * m) for m in (1, 2, 3)]
    far, last_x, *blocks = together(far, last_x, *blocks)
    low, high = across(far[:half], 1), across(last_x[half:], 2)
    came = across(jnp.stack([b[tokens:] for b in blocks]), 1)
    out = shaped((tokens, width), BF16)
    gate_grad, up_grad = call(
        outputs_body, (out, out), (spot, gate, up_proj, *blocks, came), moved=4 << 20
    )
    weight_next = in_order((own, own_x, near, near_x, last, last_x, far, low, high))
    if outer > 1:
        weight_next = (
            weight_next.reshape(CELL, outer, rows, D).transpose(1, 0, 2, 3).reshape(width, D)
        )

    def from_place(value):
        if outer == 1:
            return value
        return value.reshape(tokens, CELL, outer, rows).transpose(0, 2, 1, 3).reshape(tokens, width)

    return (
        from_place(gate_grad),
        from_place(up_grad),
        master_next,
        moment_one_next,
        moment_two_next,
        weight_next,
    )


def solution(mesh):
    n = mesh.shape["dp"]
    placed = (
        P("dp", None),
        P("dp", "tensor"),
        P("dp", "tensor"),
        P(("tensor", "dp"), None),
        P(("tensor", "dp"), None),
        P(("tensor", "dp"), None),
    )
    return jax.shard_map(
        lambda *args: on_device(n, *args),
        mesh=mesh,
        in_specs=placed,
        out_specs=(
            P("dp", "tensor"),
            P("dp", "tensor"),
            P(("tensor", "dp"), None),
            P(("tensor", "dp"), None),
            P(("tensor", "dp"), None),
            P("tensor", None),
        ),
        check_vma=False,
    )
```

```python
import jax
import jax.numpy as jnp
from jax import lax
from jax.experimental import pallas as pl
from jax.experimental.pallas import tpu as pltpu
from jax.sharding import PartitionSpec as P

D = 3072
FF = 4096
CELL = 8
BF16 = jnp.bfloat16
F32 = jnp.float32
SMEM = pl.BlockSpec(memory_space=pltpu.SMEM)
HBM = pl.BlockSpec(memory_space=pltpu.HBM)
ANY = pl.BlockSpec(memory_space=pl.ANY)
NEAR = pl.BlockSpec(memory_space=pltpu.VMEM)

MIDDLE = ((1, 2), (2, 1))
ROUND = ((0, 3), (3, 0))


def shaped(shape, dtype):
    return jax.ShapeDtypeStruct(shape, dtype)


class Near:
    def __init__(self, value):
        self.value = value


class Joined:
    def __init__(self, shape, dtype, parts):
        self.shape, self.dtype, self.parts = shape, dtype, parts


def call(body, outs, args, flops=0, moved=0, limit=24, after=()):
    spot, *args = args
    n_in, n_out = len(args), len(outs)
    flat, specs, scratch, todo = [], [], [], []

    def operand(value, spec):
        for i, old in enumerate(flat):
            if old is value and specs[i] is spec:
                return i
        flat.append(value)
        specs.append(spec)
        return len(flat) - 1

    for i, arg in enumerate(args):
        if isinstance(arg, Near):
            todo.append(operand(arg.value, NEAR))
            continue
        scratch.append(pltpu.VMEM(arg.shape, arg.dtype))
        steps = []
        for value, source, target in arg.parts if isinstance(arg, Joined) else ((arg, None, None),):
            steps.append((operand(value, ANY), source, target))
        todo.append(steps)
    count = sum(len(steps) for steps in todo if not isinstance(steps, int))

    def kernel(spot, *refs):
        given, refs = refs[: len(flat)], refs[len(flat) + len(after) :]
        results, refs = refs[:n_out], refs[n_out:]
        slots, parts = list(refs[: len(scratch)]), refs[len(scratch) : len(scratch) + n_out]
        in_sems, out_sems = refs[-2], refs[-1]
        ins, loads, used = [], {}, 0
        for i, steps in enumerate(todo):
            if isinstance(steps, int):
                ins.append(given[steps])
                continue
            ins.append(slots.pop(0))
            loads[i] = []
            for k, source, target in steps:
                copy = pltpu.make_async_copy(
                    given[k] if source is None else given[k].at[source],
                    ins[i] if target is None else ins[i].at[target],
                    in_sems.at[used],
                )
                used += 1
                copy.start()
                loads[i].append(copy)
        sent = []

        def need(*which):
            for i in which:
                for load in loads.pop(i, ()):
                    load.wait()

        def done(o, *index):
            copy = pltpu.make_async_copy(
                parts[o].at[index] if index else parts[o],
                results[o].at[index] if index else results[o],
                out_sems.at[len(sent)],
            )
            copy.start()
            sent.append(copy)

        body(spot, ins, parts, need, done)
        need(*range(n_in))
        for copy in sent:
            copy.wait()

    return pl.pallas_call(
        kernel,
        out_shape=tuple(outs),
        in_specs=[SMEM] + specs + [HBM] * len(after),
        out_specs=(HBM,) * n_out,
        scratch_shapes=scratch
        + [pltpu.VMEM(o.shape, o.dtype) for o in outs]
        + [pltpu.SemaphoreType.DMA((max(1, count),)), pltpu.SemaphoreType.DMA((32,))],
        compiler_params=pltpu.CompilerParams(vmem_limit_bytes=limit << 20),
        cost_estimate=pl.CostEstimate(flops=flops, bytes_accessed=moved, transcendentals=0),
    )(spot, *flat, *after)


def hidden_body(spot, ins, outs, need, done):
    gate, up = ins
    kept, given = outs
    z, x = spot[0], spot[1]
    part = kept.shape[1]
    need(0, 1)
    for o, out, side in ((1, given, 1 - x), (0, kept, x)):
        for m in range(4):
            cols = pl.ds(pl.multiple_of((2 * (z ^ m) + side) * part, part), part)
            gate_f = gate[:, cols].astype(F32)
            silu = gate_f * (1.0 / (1.0 + jnp.exp(-gate_f)))
            out[m] = (silu * up[:, cols].astype(F32)).T.astype(BF16)
        done(o)


def turn_body(spot, ins, outs, need, done):
    del spot
    kept, came = ins
    need(0, 1)
    for m in (3, 2, 1, 0):
        outs[m][0] = kept[m]
        outs[m][1] = came[m]
        done(m)


def tokens_in_rows(pieces):
    size, cols = pieces[0].shape
    parts = []
    for m, piece in enumerate(pieces):
        piece = piece if isinstance(piece, tuple) else (piece,)
        rows = size // len(piece)
        parts += [(p, None, (pl.ds(m * size + i * rows, rows),)) for i, p in enumerate(piece)]
    return Joined((len(pieces) * size, cols), pieces[0].dtype, parts)


def hidden_blocks(hiddens):
    shape = hiddens[0].shape
    parts = [(h, None, (i,)) for i, h in enumerate(hiddens)]
    return Joined((4,) + shape, hiddens[0].dtype, parts)


def grad_body(spot, ins, outs, need, done):
    del spot
    hidden, pieces = ins
    part, size = hidden.shape[-2:]
    need(0, 1)
    total = None
    for m in range(CELL):
        left = jnp.concatenate([hidden[i, m // 2, m % 2] for i in range(4)], axis=0)
        right = pieces[m * size : (m + 1) * size, :]
        term = jnp.dot(left, right, preferred_element_type=F32)
        total = term if total is None else total + term
    for i in (3, 2, 1, 0):
        outs[i][...] = total[i * part : (i + 1) * part].astype(outs[i].dtype)
        done(i)
    outs[4][...] = jnp.broadcast_to(jnp.sum(total * total), outs[4].shape)
    done(4)


def d_hidden_body(spot, ins, outs, need, done):
    del spot
    pieces, weights = ins
    keep, give = outs
    part = weights.shape[0] // 4
    tokens = pieces.shape[0] // CELL
    need(0, 1)
    weight = weights[...].T
    for m in range(CELL):
        at = pl.ds(m * tokens, tokens)
        out = jnp.dot(pieces[at, :], weight, preferred_element_type=F32)
        for i, into in ((1, give), (3, give), (0, keep), (2, keep)):
            into[i // 2, at] = out[:, i * part : (i + 1) * part]
        done(1, slice(None), at)
        done(0, slice(None), at)


def add_body(spot, ins, outs, need, done):
    del spot
    keep, give = ins
    mine, sent = outs
    need(0, 1)
    sent[...] = keep[1] + give[1]
    done(1)
    mine[...] = keep[0] + give[0]
    done(0)


def back_body(spot, ins, outs, need, done):
    del spot
    mine, came = ins
    rows = outs[0].shape[0]
    need(0, 1)
    for m in (3, 2, 1, 0):
        at = slice(m * rows, (m + 1) * rows)
        outs[m][...] = (mine[at] + came[at]).astype(BF16)
        done(m)


def adam_body(spot, ins, outs, need, done):
    total, grads = ins[0], ins[1:5]
    master, one, two = ins[5:]
    master_next, one_next, two_next, shard = outs
    t = spot[2]
    cols = grads[0].shape[1]
    need(0)
    factor = 1.0 / jnp.sqrt(total[0:1, 0:1] / (FF * D) + 1e-06)
    need(5, 6, 7)
    for m, g in enumerate(grads):
        need(1 + m)
        at = pl.ds(pl.multiple_of((t ^ m) * cols, cols), cols)
        clipped = g[...].astype(F32) * factor
        first = 0.9 * one[:, at] + 0.1 * clipped
        second = 0.95 * two[:, at] + 0.05 * clipped * clipped
        old = master[:, at]
        new = old - 0.003 * (first / (jnp.sqrt(second) + 1e-08) + 0.1 * old)
        one_next[:, at] = first
        two_next[:, at] = second
        master_next[:, at] = new
        shard[:, at] = new.astype(BF16)
        for o in (3, 0, 1, 2):
            done(o, slice(None), at)


def outputs_body(spot, ins, outs, need, done):
    gate, up, *blocks, came = ins
    gate_grad, up_grad = outs
    z, x = spot[0], spot[1]
    tokens, part = came.shape[1:]
    need(*range(7))
    for m, block in enumerate(blocks):
        for side in range(2):
            d_hidden = (came[m] if side else block[:tokens]).astype(F32)
            cols = pl.ds(pl.multiple_of((2 * (z ^ m) + (x ^ side)) * part, part), part)
            gate_f = gate[:, cols].astype(F32)
            sigm = 1.0 / (1.0 + jnp.exp(-gate_f))
            up_grad[:, cols] = (d_hidden * (gate_f * sigm)).astype(BF16)
            gate_grad[:, cols] = (
                d_hidden * up[:, cols].astype(F32) * sigm * (1.0 + gate_f * (1.0 - sigm))
            ).astype(BF16)
    done(0)
    done(1)


def gate_body(*refs):
    del refs


def together(*values, after=()):
    return pl.pallas_call(
        gate_body,
        out_shape=tuple(shaped(v.shape, v.dtype) for v in values),
        in_specs=[HBM] * len(values) + [ANY] * len(after),
        out_specs=(HBM,) * len(values),
        input_output_aliases={i: i for i in range(len(values))},
        compiler_params=pltpu.CompilerParams(vmem_limit_bytes=8 << 20),
    )(*values, *after)


def on_device(n, d_out, gate, up_proj, master, moment_one, moment_two):
    outer = n // CELL
    place = lax.axis_index("dp")
    z, x = place % CELL // 2, place % 2
    t = lax.axis_index("tensor")
    spot = jnp.stack([z, x, t]).astype(jnp.int32)
    tokens, width = gate.shape
    rows = master.shape[0]
    part = width // CELL
    cols = D // 4
    same_pair = [[k + CELL * j for j in range(outer)] for k in range(CELL)]

    def across(value, m):
        return lax.ppermute(value, "dp", [(i, i ^ m) for i in range(n)])

    def line(value, pairs):
        steps = [(i, b) for i in range(n) for a, b in pairs if i % CELL // 2 == a]
        return lax.ppermute(value, "dp", [(i, i - i % CELL + b * 2 + i % 2) for i, b in steps])

    def swap(value, m):
        return lax.ppermute(value, "tensor", [(i, i ^ m) for i in range(4)])

    def in_order(pieces):
        own, own_x, near, near_x, last, last_x, far, low, high = pieces
        size, half = own.shape[0], low.shape[0]
        out = jnp.zeros((CELL * size,) + own.shape[1:], own.dtype)
        for value, m, shift in (
            (own, 0, 0), (own_x, 1, 0), (near, 2, 0), (near_x, 3, 0), (last, 6, 0),
            (last_x, 7, 0), (far, 4, 0), (low, 5, 0), (high, 5, half),
        ):
            at = (place % CELL ^ m) * size + shift
            out = lax.dynamic_update_slice(out, value, (at, 0))
        return out

    def by_place(value):
        if outer == 1:
            return value
        return value.reshape(tokens, outer, CELL, rows).transpose(0, 2, 1, 3).reshape(tokens, width)

    gate, up_proj = by_place(gate), by_place(up_proj)

    own = lax.dynamic_slice(d_out, (0, t * cols), (tokens, cols))
    half = tokens // 2
    ends = (z == 0) | (z == 3)
    near, own_x, mid = across(own, 2), across(own, 1), line(own, MIDDLE)
    block = shaped((4, part, tokens), BF16)
    kept, given = call(hidden_body, (block, block), (spot, gate, up_proj), moved=2 << 20)
    near, own_x, mid, given, own = together(near, own_x, mid, given, own)
    end, near_x, came = line(own, ROUND), across(near, 1), across(given, 1)
    end, came = together(end, came, after=(near_x,))
    last = jnp.where(ends, end, mid)
    far, last_x = across(last, 2), across(last, 1)
    pair = shaped((2, part, tokens), BF16)
    blocks = call(turn_body, (pair,) * 4, (spot, kept, came), moved=1 << 20)
    blocks = [blocks[0]] + [across(blocks[m], 2 * m) for m in (1, 2, 3)]
    far, last_x, *blocks = together(far, last_x, *blocks)
    low, high = across(far[:half], 1), across(last_x[half:], 2)
    hidden = jnp.stack(blocks)
    hidden_y, hidden_c = swap(hidden, 2), swap(hidden, 1)
    (hidden_y,) = together(hidden_y, after=(low, high))
    hiddens = (hidden, hidden_c, hidden_y, swap(hidden_y, 1))
    weight = master
    if outer > 1:
        weight = lax.all_gather(
            master.astype(BF16), "dp", axis=0, tiled=True, axis_index_groups=same_pair
        )
    weights = [
        lax.dynamic_slice(weight, (0, (t ^ m) * cols), (part, cols)).astype(BF16) for m in range(4)
    ]
    weights = [weights[0]] + [swap(weights[m], m) for m in (1, 2, 3)]
    pieces = tokens_in_rows((own, own_x, near, near_x, far, (low, high), last, last_x))

    flops = 2 * 4 * part * CELL * tokens * cols
    piece, sent = shaped((part, cols), F32), shaped((part, cols), BF16)
    *grads, total = call(
        grad_body,
        (piece, sent, sent, sent, shaped((8, 128), F32)),
        (spot, hidden_blocks(hiddens), pieces),
        flops=flops,
        moved=8 << 20,
        limit=52,
    )
    if outer > 1:
        grads = lax.psum_scatter(
            jnp.stack([g.astype(F32) for g in grads]).reshape(4, outer, rows, cols),
            "dp",
            scatter_dimension=1,
            axis_index_groups=same_pair,
        )
        total = jnp.broadcast_to(jnp.sum(grads * grads), (8, 128))
    grad_own = grads[0]
    step = 1
    while step < n:
        total = total + across(total, step)
        step *= 2
    for m in (1, 2):
        total = total + swap(total, m)
    grads = [grads[0]] + [swap(grads[m], m) for m in (1, 2, 3)]

    sums = shaped((2, CELL * tokens, part), F32)
    weights = Joined(
        (4 * part, cols), BF16, [(w, None, (pl.ds(m * part, part),)) for m, w in enumerate(weights)]
    )
    keep, give = call(
        d_hidden_body,
        (sums, sums),
        (spot, pieces, weights),
        flops=flops,
        moved=10 << 20,
        limit=52,
        after=(grad_own,),
    )
    give = swap(give, 1)

    state = shaped((rows, D), F32)
    master_next, moment_one_next, moment_two_next, shard_next = call(
        adam_body,
        (state, state, state, shaped((rows, D), BF16)),
        (spot, total, *grads, master, moment_one, moment_two),
        moved=12 << 20,
    )
    if outer > 1:
        shard_next = lax.all_gather(
            shard_next, "dp", axis=0, tiled=True, axis_index_groups=same_pair
        )
    own = shard_next
    half = own.shape[0] // 2
    near, own_x, mid = across(own, 2), across(own, 1), line(own, MIDDLE)
    mine_sum = shaped((CELL * tokens, part), F32)
    mine, sent = call(add_body, (mine_sum,) * 2, (spot, keep, give), moved=6 << 20)
    near, own_x, mid, sent, own = together(near, own_x, mid, sent, own)
    end, near_x, came = line(own, ROUND), across(near, 1), swap(sent, 2)
    end, near_x = together(end, near_x)
    last = jnp.where(ends, end, mid)
    far, last_x = across(last, 2), across(last, 1)
    pair = shaped((2 * tokens, part), BF16)
    blocks = call(back_body, (pair,) * 4, (spot, mine, came), moved=3 << 20)
    blocks = [blocks[0]] + [across(blocks[m], 2 * m) for m in (1, 2, 3)]
    far, last_x, *blocks = together(far, last_x, *blocks)
    given = jnp.stack([b[tokens:] for b in blocks])
    far, last_x = together(far, last_x, after=(given,))
    came = across(given, 1)
    low, high = across(far[:half], 1), across(last_x[half:], 2)
    out = shaped((tokens, width), BF16)
    gate_grad, up_grad = call(
        outputs_body, (out, out), (spot, gate, up_proj, *blocks, came), moved=4 << 20
    )
    weight_next = in_order((own, own_x, near, near_x, last, last_x, far, low, high))
    if outer > 1:
        weight_next = (
            weight_next.reshape(CELL, outer, rows, D).transpose(1, 0, 2, 3).reshape(width, D)
        )

    def from_place(value):
        if outer == 1:
            return value
        return value.reshape(tokens, CELL, outer, rows).transpose(0, 2, 1, 3).reshape(tokens, width)

    return (
        from_place(gate_grad),
        from_place(up_grad),
        master_next,
        moment_one_next,
        moment_two_next,
        weight_next,
    )


def solution(mesh):
    n = mesh.shape["dp"]
    placed = (
        P("dp", None),
        P("dp", "tensor"),
        P("dp", "tensor"),
        P(("tensor", "dp"), None),
        P(("tensor", "dp"), None),
        P(("tensor", "dp"), None),
    )
    return jax.shard_map(
        lambda *args: on_device(n, *args),
        mesh=mesh,
        in_specs=placed,
        out_specs=(
            P("dp", "tensor"),
            P("dp", "tensor"),
            P(("tensor", "dp"), None),
            P(("tensor", "dp"), None),
            P(("tensor", "dp"), None),
            P("tensor", None),
        ),
        check_vma=False,
    )
```

```python
import jax
import jax.numpy as jnp
from jax import lax
from jax.experimental import pallas as pl
from jax.experimental.pallas import tpu as pltpu
from jax.sharding import PartitionSpec as P

D = 3072
FF = 4096
CELL = 8
BF16 = jnp.bfloat16
F32 = jnp.float32
SMEM = pl.BlockSpec(memory_space=pltpu.SMEM)
HBM = pl.BlockSpec(memory_space=pltpu.HBM)
ANY = pl.BlockSpec(memory_space=pl.ANY)
NEAR = pl.BlockSpec(memory_space=pltpu.VMEM)

MIDDLE = ((1, 2), (2, 1))
ROUND = ((0, 3), (3, 0))


def shaped(shape, dtype):
    return jax.ShapeDtypeStruct(shape, dtype)


class Near:
    def __init__(self, value):
        self.value = value


class Joined:
    def __init__(self, shape, dtype, parts):
        self.shape, self.dtype, self.parts = shape, dtype, parts


def call(body, outs, args, flops=0, moved=0, limit=24, after=()):
    spot, *args = args
    n_in, n_out = len(args), len(outs)
    flat, specs, scratch, todo = [], [], [], []

    def operand(value, spec):
        for i, old in enumerate(flat):
            if old is value and specs[i] is spec:
                return i
        flat.append(value)
        specs.append(spec)
        return len(flat) - 1

    for i, arg in enumerate(args):
        if isinstance(arg, Near):
            todo.append(operand(arg.value, NEAR))
            continue
        scratch.append(pltpu.VMEM(arg.shape, arg.dtype))
        steps = []
        for value, source, target in arg.parts if isinstance(arg, Joined) else ((arg, None, None),):
            steps.append((operand(value, ANY), source, target))
        todo.append(steps)
    count = sum(len(steps) for steps in todo if not isinstance(steps, int))

    def kernel(spot, *refs):
        given, refs = refs[: len(flat)], refs[len(flat) + len(after) :]
        results, refs = refs[:n_out], refs[n_out:]
        slots, parts = list(refs[: len(scratch)]), refs[len(scratch) : len(scratch) + n_out]
        in_sems, out_sems = refs[-2], refs[-1]
        ins, loads, used = [], {}, 0
        for i, steps in enumerate(todo):
            if isinstance(steps, int):
                ins.append(given[steps])
                continue
            ins.append(slots.pop(0))
            loads[i] = []
            for k, source, target in steps:
                copy = pltpu.make_async_copy(
                    given[k] if source is None else given[k].at[source],
                    ins[i] if target is None else ins[i].at[target],
                    in_sems.at[used],
                )
                used += 1
                copy.start()
                loads[i].append(copy)
        sent = []

        def need(*which):
            for i in which:
                for load in loads.pop(i, ()):
                    load.wait()

        def done(o, *index):
            copy = pltpu.make_async_copy(
                parts[o].at[index] if index else parts[o],
                results[o].at[index] if index else results[o],
                out_sems.at[len(sent)],
            )
            copy.start()
            sent.append(copy)

        body(spot, ins, parts, need, done)
        need(*range(n_in))
        for copy in sent:
            copy.wait()

    return pl.pallas_call(
        kernel,
        out_shape=tuple(outs),
        in_specs=[SMEM] + specs + [HBM] * len(after),
        out_specs=(HBM,) * n_out,
        scratch_shapes=scratch
        + [pltpu.VMEM(o.shape, o.dtype) for o in outs]
        + [pltpu.SemaphoreType.DMA((max(1, count),)), pltpu.SemaphoreType.DMA((32,))],
        compiler_params=pltpu.CompilerParams(vmem_limit_bytes=limit << 20),
        cost_estimate=pl.CostEstimate(flops=flops, bytes_accessed=moved, transcendentals=0),
    )(spot, *flat, *after)


def hidden_body(spot, ins, outs, need, done):
    gate, up = ins
    kept, given = outs
    z, x = spot[0], spot[1]
    part = kept.shape[1]
    need(0, 1)
    for o, out, side in ((1, given, 1 - x), (0, kept, x)):
        for m in range(4):
            cols = pl.ds(pl.multiple_of((2 * (z ^ m) + side) * part, part), part)
            gate_f = gate[:, cols].astype(F32)
            silu = gate_f * (1.0 / (1.0 + jnp.exp(-gate_f)))
            out[m] = (silu * up[:, cols].astype(F32)).T.astype(BF16)
        done(o)


def turn_body(spot, ins, outs, need, done):
    del spot
    kept, came = ins
    need(0, 1)
    for m in (3, 2, 1, 0):
        outs[m][0] = kept[m]
        outs[m][1] = came[m]
        done(m)


def tokens_in_rows(pieces):
    size, cols = pieces[0].shape
    parts = []
    for m, piece in enumerate(pieces):
        piece = piece if isinstance(piece, tuple) else (piece,)
        rows = size // len(piece)
        parts += [(p, None, (pl.ds(m * size + i * rows, rows),)) for i, p in enumerate(piece)]
    return Joined((len(pieces) * size, cols), pieces[0].dtype, parts)


def hidden_blocks(hiddens):
    shape = hiddens[0].shape
    parts = [(h, None, (i,)) for i, h in enumerate(hiddens)]
    return Joined((4,) + shape, hiddens[0].dtype, parts)


def grad_body(spot, ins, outs, need, done):
    del spot
    hidden, pieces = ins
    part, size = hidden.shape[-2:]
    need(0, 1)
    total = None
    for m in range(CELL):
        left = jnp.concatenate([hidden[i, m // 2, m % 2] for i in range(4)], axis=0)
        right = pieces[m * size : (m + 1) * size, :]
        term = jnp.dot(left, right, preferred_element_type=F32)
        total = term if total is None else total + term
    for i in (3, 2, 1, 0):
        outs[i][...] = total[i * part : (i + 1) * part].astype(outs[i].dtype)
        done(i)
    outs[4][...] = jnp.broadcast_to(jnp.sum(total * total), outs[4].shape)
    done(4)


def d_hidden_body(spot, ins, outs, need, done):
    del spot
    pieces, weights = ins
    keep, give = outs
    part = weights.shape[0] // 4
    tokens = pieces.shape[0] // CELL
    need(0, 1)
    weight = weights[...].T
    for m in range(CELL):
        at = pl.ds(m * tokens, tokens)
        out = jnp.dot(pieces[at, :], weight, preferred_element_type=F32)
        for i, into in ((1, give), (3, give), (0, keep), (2, keep)):
            into[i // 2, at] = out[:, i * part : (i + 1) * part]
        done(1, slice(None), at)
        done(0, slice(None), at)


def add_body(spot, ins, outs, need, done):
    del spot
    keep, give = ins
    mine, sent = outs
    need(0, 1)
    sent[...] = keep[1] + give[1]
    done(1)
    mine[...] = keep[0] + give[0]
    done(0)


def back_body(spot, ins, outs, need, done):
    del spot
    mine, came = ins
    rows = outs[0].shape[0]
    need(0, 1)
    for m in (3, 2, 1, 0):
        at = slice(m * rows, (m + 1) * rows)
        outs[m][...] = (mine[at] + came[at]).astype(BF16)
        done(m)


def adam_body(spot, ins, outs, need, done):
    total, grads = ins[0], ins[1:5]
    master, one, two = ins[5:]
    master_next, one_next, two_next, shard = outs
    t = spot[2]
    cols = grads[0].shape[1]
    need(0)
    factor = 1.0 / jnp.sqrt(total[0:1, 0:1] / (FF * D) + 1e-06)
    need(5, 6, 7)
    for m, g in enumerate(grads):
        need(1 + m)
        at = pl.ds(pl.multiple_of((t ^ m) * cols, cols), cols)
        clipped = g[...].astype(F32) * factor
        first = 0.9 * one[:, at] + 0.1 * clipped
        second = 0.95 * two[:, at] + 0.05 * clipped * clipped
        old = master[:, at]
        new = old - 0.003 * (first / (jnp.sqrt(second) + 1e-08) + 0.1 * old)
        one_next[:, at] = first
        two_next[:, at] = second
        master_next[:, at] = new
        shard[:, at] = new.astype(BF16)
        for o in (3, 0, 1, 2):
            done(o, slice(None), at)


def outputs_body(spot, ins, outs, need, done):
    gate, up, *blocks, came = ins
    gate_grad, up_grad = outs
    z, x = spot[0], spot[1]
    tokens, part = came.shape[1:]
    need(*range(7))
    for m, block in enumerate(blocks):
        for side in range(2):
            d_hidden = (came[m] if side else block[:tokens]).astype(F32)
            cols = pl.ds(pl.multiple_of((2 * (z ^ m) + (x ^ side)) * part, part), part)
            gate_f = gate[:, cols].astype(F32)
            sigm = 1.0 / (1.0 + jnp.exp(-gate_f))
            up_grad[:, cols] = (d_hidden * (gate_f * sigm)).astype(BF16)
            gate_grad[:, cols] = (
                d_hidden * up[:, cols].astype(F32) * sigm * (1.0 + gate_f * (1.0 - sigm))
            ).astype(BF16)
    done(0)
    done(1)


def gate_body(*refs):
    del refs


def together(*values, after=()):
    return pl.pallas_call(
        gate_body,
        out_shape=tuple(shaped(v.shape, v.dtype) for v in values),
        in_specs=[HBM] * len(values) + [ANY] * len(after),
        out_specs=(HBM,) * len(values),
        input_output_aliases={i: i for i in range(len(values))},
        compiler_params=pltpu.CompilerParams(vmem_limit_bytes=8 << 20),
    )(*values, *after)


def on_device(n, d_out, gate, up_proj, master, moment_one, moment_two):
    outer = n // CELL
    place = lax.axis_index("dp")
    z, x = place % CELL // 2, place % 2
    t = lax.axis_index("tensor")
    spot = jnp.stack([z, x, t]).astype(jnp.int32)
    tokens, width = gate.shape
    rows = master.shape[0]
    part = width // CELL
    cols = D // 4
    same_pair = [[k + CELL * j for j in range(outer)] for k in range(CELL)]

    def across(value, m):
        return lax.ppermute(value, "dp", [(i, i ^ m) for i in range(n)])

    def line(value, pairs):
        steps = [(i, b) for i in range(n) for a, b in pairs if i % CELL // 2 == a]
        return lax.ppermute(value, "dp", [(i, i - i % CELL + b * 2 + i % 2) for i, b in steps])

    def swap(value, m):
        return lax.ppermute(value, "tensor", [(i, i ^ m) for i in range(4)])

    def in_order(pieces):
        own, own_x, near, near_x, last, last_x, far, low, high = pieces
        size, half = own.shape[0], low.shape[0]
        out = jnp.zeros((CELL * size,) + own.shape[1:], own.dtype)
        for value, m, shift in (
            (own, 0, 0), (own_x, 1, 0), (near, 2, 0), (near_x, 3, 0), (last, 6, 0),
            (last_x, 7, 0), (far, 4, 0), (low, 5, 0), (high, 5, half),
        ):
            at = (place % CELL ^ m) * size + shift
            out = lax.dynamic_update_slice(out, value, (at, 0))
        return out

    def by_place(value):
        if outer == 1:
            return value
        return value.reshape(tokens, outer, CELL, rows).transpose(0, 2, 1, 3).reshape(tokens, width)

    gate, up_proj = by_place(gate), by_place(up_proj)

    own = lax.dynamic_slice(d_out, (0, t * cols), (tokens, cols))
    half = tokens // 2
    ends = (z == 0) | (z == 3)
    near, own_x, mid = across(own, 2), across(own, 1), line(own, MIDDLE)
    block = shaped((4, part, tokens), BF16)
    kept, given = call(hidden_body, (block, block), (spot, gate, up_proj), moved=2 << 20)
    near, own_x, mid, given, own = together(near, own_x, mid, given, own)
    end, near_x, came = line(own, ROUND), across(near, 1), across(given, 1)
    end, came = together(end, came, after=(near_x,))
    last = jnp.where(ends, end, mid)
    far, last_x = across(last, 2), across(last, 1)
    pair = shaped((2, part, tokens), BF16)
    blocks = call(turn_body, (pair,) * 4, (spot, kept, came), moved=1 << 20)
    blocks = [blocks[0]] + [across(blocks[m], 2 * m) for m in (1, 2, 3)]
    far, last_x, *blocks = together(far, last_x, *blocks)
    low, high = across(far[:half], 1), across(last_x[half:], 2)
    hidden = jnp.stack(blocks)
    hidden_y, hidden_c = swap(hidden, 2), swap(hidden, 1)
    (hidden_y,) = together(hidden_y, after=(low, high))
    hiddens = (hidden, hidden_c, hidden_y, swap(hidden_y, 1))
    weight = master
    if outer > 1:
        weight = lax.all_gather(
            master.astype(BF16), "dp", axis=0, tiled=True, axis_index_groups=same_pair
        )
    weights = [
        lax.dynamic_slice(weight, (0, (t ^ m) * cols), (part, cols)).astype(BF16) for m in range(4)
    ]
    weights = [weights[0]] + [swap(weights[m], m) for m in (1, 2, 3)]
    pieces = tokens_in_rows((own, own_x, near, near_x, far, (low, high), last, last_x))

    flops = 2 * 4 * part * CELL * tokens * cols
    piece, sent = shaped((part, cols), F32), shaped((part, cols), BF16)
    *grads, total = call(
        grad_body,
        (piece, sent, sent, sent, shaped((8, 128), F32)),
        (spot, hidden_blocks(hiddens), pieces),
        flops=flops,
        moved=8 << 20,
        limit=52,
    )
    if outer > 1:
        grads = lax.psum_scatter(
            jnp.stack([g.astype(F32) for g in grads]).reshape(4, outer, rows, cols),
            "dp",
            scatter_dimension=1,
            axis_index_groups=same_pair,
        )
        total = jnp.broadcast_to(jnp.sum(grads * grads), (8, 128))
    grad_own = grads[0]
    step = 1
    while step < n:
        total = total + across(total, step)
        step *= 2
    for m in (1, 2):
        total = total + swap(total, m)
    grads = [grads[0]] + [swap(grads[m], m) for m in (1, 2, 3)]

    sums = shaped((2, CELL * tokens, part), F32)
    weights = Joined(
        (4 * part, cols), BF16, [(w, None, (pl.ds(m * part, part),)) for m, w in enumerate(weights)]
    )
    keep, give = call(
        d_hidden_body,
        (sums, sums),
        (spot, pieces, weights),
        flops=flops,
        moved=10 << 20,
        limit=52,
        after=(grad_own,),
    )
    give = swap(give, 1)

    state = shaped((rows, D), F32)
    master_next, moment_one_next, moment_two_next, shard_next = call(
        adam_body,
        (state, state, state, shaped((rows, D), BF16)),
        (spot, total, *grads, master, moment_one, moment_two),
        moved=12 << 20,
    )
    if outer > 1:
        shard_next = lax.all_gather(
            shard_next, "dp", axis=0, tiled=True, axis_index_groups=same_pair
        )
    own = shard_next
    half = own.shape[0] // 2
    near, own_x, mid = across(own, 2), across(own, 1), line(own, MIDDLE)
    mine_sum = shaped((CELL * tokens, part), F32)
    mine, sent = call(add_body, (mine_sum,) * 2, (spot, keep, give), moved=6 << 20)
    near, own_x, mid, own = together(near, own_x, mid, own, after=(sent,))
    end, near_x, came = line(own, ROUND), across(near, 1), swap(sent, 2)
    end, near_x = together(end, near_x)
    last = jnp.where(ends, end, mid)
    far, last_x = across(last, 2), across(last, 1)
    pair = shaped((2 * tokens, part), BF16)
    blocks = call(back_body, (pair,) * 4, (spot, mine, came), moved=3 << 20)
    blocks = [blocks[0]] + [across(blocks[m], 2 * m) for m in (1, 2, 3)]
    far, last_x, *blocks = together(far, last_x, *blocks)
    given = jnp.stack([b[tokens:] for b in blocks])
    far, last_x = together(far, last_x, after=(given,))
    came = across(given, 1)
    low, high = across(far[:half], 1), across(last_x[half:], 2)
    out = shaped((tokens, width), BF16)
    gate_grad, up_grad = call(
        outputs_body, (out, out), (spot, gate, up_proj, *blocks, came), moved=4 << 20
    )
    weight_next = in_order((own, own_x, near, near_x, last, last_x, far, low, high))
    if outer > 1:
        weight_next = (
            weight_next.reshape(CELL, outer, rows, D).transpose(1, 0, 2, 3).reshape(width, D)
        )

    def from_place(value):
        if outer == 1:
            return value
        return value.reshape(tokens, CELL, outer, rows).transpose(0, 2, 1, 3).reshape(tokens, width)

    return (
        from_place(gate_grad),
        from_place(up_grad),
        master_next,
        moment_one_next,
        moment_two_next,
        weight_next,
    )


def solution(mesh):
    n = mesh.shape["dp"]
    placed = (
        P("dp", None),
        P("dp", "tensor"),
        P("dp", "tensor"),
        P(("tensor", "dp"), None),
        P(("tensor", "dp"), None),
        P(("tensor", "dp"), None),
    )
    return jax.shard_map(
        lambda *args: on_device(n, *args),
        mesh=mesh,
        in_specs=placed,
        out_specs=(
            P("dp", "tensor"),
            P("dp", "tensor"),
            P(("tensor", "dp"), None),
            P(("tensor", "dp"), None),
            P(("tensor", "dp"), None),
            P("tensor", None),
        ),
        check_vma=False,
    )
```
